32 devices in a mesh: groups: 2 (over x), heads: 8 (over z, y), query: 2 (over core).
Axes of the slice: x: 2, y: 2, z: 4, core: 2. Of those that a mesh axis runs over, the one named last changes fastest.
Arguments:
- q_compressed: bfloat16 [256, 1536], P(('groups', 'heads', 'query')), parts along dimension 0, may hold values from -6 to 6
- new_latent: bfloat16 [256, 576], P(('groups', 'heads', 'query')), parts along dimension 0, may hold values from -6 to 6
- cached_latent: bfloat16 [2048, 576], P(('groups', 'heads', 'query')), parts along dimension 0
- latent_gain: float32 [512], replicated, may hold values from 0.1 to 1.9
- cached_length: int32 [2], P('groups'), parts along dimension 0, may hold values from 1 to 1024, as said below
- w_q_nope: bfloat16 [1536, 4096], P(None, 'heads'), may hold values from -0.15625 to 0.15625
- w_q_rope: bfloat16 [1536, 2048], P(None, 'heads'), may hold values from -0.15625 to 0.15625
- w_uk: bfloat16 [512, 4096], P(None, 'heads'), may hold values from -0.25 to 0.25
- w_uv: bfloat16 [512, 4096], P(None, 'heads'), may hold values from -0.25 to 0.25
- w_out: bfloat16 [4096, 7168], P('heads'), may hold values from -0.75 to 0.75
Outputs:
- attended: bfloat16 [256, 7168], P(('groups', 'heads', 'query')), parts along dimension 0
The draws below stay inside these ranges and needn't reach their ends.
There are 2 independent parts, one for each index of `groups`. The reference program is written for one: setup_inputs(seed, part) draws one part's arguments, and reference() takes and returns one part's arrays. A program takes and returns all parts, laid end to end along the dimension named above; an argument that names none is the same for every part. Nothing has to cross between parts.
Inputs may be any that keep to these rules, and one draw needn't show every extreme that they name: `cached_length`: live cache slots; the span follows them.
All inputs are finite; a program needn't handle non-finite values.
Results may differ from the reference program's by a relative error of at most 0.014.
The reference program's roundings to bfloat16 on the way count: a program that leaves them out, or rounds other values in their place, can miss the bound.
Values may be sent and summed in bfloat16 or wider, within the bound.
A program may use at most 128 MiB of HBM per device.

```python
import jax
import jax.numpy as jnp
from jax import lax

D = 7168
QR = 1536
KR = 512
RD = 64
ND = 128
VD = 128
HEADS_DEV = 4
H = 32
SPAN = 128
CTX = 1024


def draw_cached_latent(key, part):
    key = jax.random.fold_in(key, 11)
    first, second = jax.random.split(key)
    latent = jax.random.normal(first, (CTX, KR), jnp.float32)
    turned = jax.random.normal(second, (CTX, RD), jnp.float32)
    return jnp.concatenate([latent, turned], axis=-1).astype(jnp.bfloat16)


def draw_cached_length(key, part):
    key = jax.random.fold_in(key, 5)
    drawn = jax.random.randint(key, (1,), 1, CTX + 1)
    return jnp.where(part == 1, CTX, drawn).astype(jnp.int32)


def block_levels(own_key, extent, cuts, low, top_value):
    level, own = 1.0, jax.random.fold_in(own_key, 6)
    for position, shards_of in cuts:
        draws = jnp.exp(jax.random.uniform(jax.random.fold_in(own, position), (shards_of,), jnp.float32, low / len(cuts), top_value / len(cuts)))
        level = level * jnp.repeat(draws, extent[position] // shards_of).reshape([-1 if axis == position else 1 for axis in range(len(extent))])
    return level


def normal_values(own_key, extent, scale, bound, cuts=(), kind=jnp.bfloat16):
    factor_of = block_levels(own_key, extent, cuts, -0.22, 0.18) if cuts else 1.0
    result = jax.random.normal(own_key, extent, jnp.float32) * scale * factor_of
    return jnp.minimum(jnp.maximum(result, -bound), bound).astype(kind)


def setup_inputs(seed: int = 0, part: int = 0) -> dict:
    streams_of = jax.random.split(jax.random.key(seed), 11)
    own_keys = jax.random.split(jax.random.fold_in(streams_of[10], part), 11)
    return {
        "q_compressed": normal_values(own_keys[0], (SPAN, QR), 1.0, 6.0, ((0, 16),)),
        "new_latent": normal_values(own_keys[1], (SPAN, KR + RD), 1.0, 6.0, ((0, 16),)),
        "cached_latent": draw_cached_latent(jax.random.fold_in(jax.random.fold_in(streams_of[10], part), 71), part),
        "latent_gain": jnp.clip(1.0 + 0.18 * jax.random.normal(streams_of[3], (KR,), jnp.float32), 0.1, 1.9),
        "cached_length": draw_cached_length(jax.random.fold_in(jax.random.fold_in(streams_of[10], part), 71), part),
        "w_q_nope": normal_values(streams_of[5], (QR, H * ND), QR ** -0.5, 0.15625, ((1, 8),)),
        "w_q_rope": normal_values(streams_of[6], (QR, H * RD), QR ** -0.5, 0.15625, ((1, 8),)),
        "w_uk": normal_values(streams_of[7], (KR, H * ND), KR ** -0.5, 0.25, ((1, 8),)),
        "w_uv": normal_values(streams_of[8], (KR, H * VD), KR ** -0.5, 0.25, ((1, 8),)),
        "w_out": normal_values(streams_of[9], (H * VD, D), 0.125, 0.75, ((0, 8),)),
    }


def rotate(vectors, positions):
    half = vectors.shape[-1] // 2
    freq = 10000.0 ** (-2.0 * jnp.arange(half, dtype=jnp.float32) / vectors.shape[-1])
    angle = positions.astype(jnp.float32)[:, None] * freq[None, :]
    while angle.ndim < vectors.ndim:
        angle = angle[:, None, :]
    first = vectors[..., :half]
    second = vectors[..., half:]
    return jnp.concatenate([first * jnp.cos(angle) - second * jnp.sin(angle), second * jnp.cos(angle) + first * jnp.sin(angle)], axis=-1)

def normalize_new(raw, gain, positions):
    latent = raw[:, :KR].astype(jnp.float32)
    latent = latent * lax.rsqrt(lax.optimization_barrier(jnp.mean(latent * latent, axis=-1, keepdims=True)) + 1e-06) * gain
    turned = rotate(raw[:, KR:].astype(jnp.float32), positions)
    return jnp.concatenate([latent, turned], axis=-1).astype(jnp.bfloat16)

def reference(q_compressed, new_latent, cached_latent, latent_gain, cached_length, w_q_nope, w_q_rope, w_uk, w_uv, w_out):
    ctx_len = cached_length[0]
    tokens = jnp.arange(SPAN, dtype=jnp.int32)
    fresh = normalize_new(new_latent, latent_gain, ctx_len + tokens)
    keys = jnp.concatenate([cached_latent, fresh], axis=0)
    kidx = jnp.arange(CTX + SPAN, dtype=jnp.int32)[None, :]
    live = jnp.where(kidx < CTX, kidx < ctx_len, kidx - CTX <= tokens[:, None])
    scale = (ND + RD) ** (-0.5)
    keys_f = keys.astype(jnp.float32)
    latents_f = keys_f[:, :KR]

    def block(total, index):
        wqn = lax.dynamic_slice_in_dim(w_q_nope, index * HEADS_DEV * ND, HEADS_DEV * ND, 1)
        wqr = lax.dynamic_slice_in_dim(w_q_rope, index * HEADS_DEV * RD, HEADS_DEV * RD, 1)
        wuk = lax.dynamic_slice_in_dim(w_uk, index * HEADS_DEV * ND, HEADS_DEV * ND, 1)
        wuv = lax.dynamic_slice_in_dim(w_uv, index * HEADS_DEV * VD, HEADS_DEV * VD, 1)
        wout = lax.dynamic_slice_in_dim(w_out, index * HEADS_DEV * VD, HEADS_DEV * VD, 0)
        q_nope = jnp.dot(q_compressed, wqn, preferred_element_type=jnp.float32).astype(jnp.bfloat16)
        q_rope = jnp.dot(q_compressed, wqr, preferred_element_type=jnp.float32).reshape(SPAN, HEADS_DEV, RD)
        q_rope = rotate(q_rope, ctx_len + tokens).astype(jnp.bfloat16)
        q_lat = jnp.einsum('thd,khd->htk', q_nope.reshape(SPAN, HEADS_DEV, ND).astype(jnp.float32), wuk.reshape(KR, HEADS_DEV, ND).astype(jnp.float32)).astype(jnp.bfloat16)
        q_all = jnp.concatenate([q_lat, jnp.transpose(q_rope, (1, 0, 2))], axis=-1).astype(jnp.float32)
        scores = jnp.einsum('htc,kc->htk', q_all, keys_f) * scale
        scores = jnp.where(live[None, :, :], scores, -1e+30)
        top = lax.optimization_barrier(jnp.max(scores, axis=-1, keepdims=True))
        expo = jnp.exp(scores - top)
        weights = (expo / lax.optimization_barrier(jnp.sum(expo, axis=-1, keepdims=True))).astype(jnp.bfloat16)
        o_lat = jnp.einsum('htk,kc->htc', weights.astype(jnp.float32), latents_f).astype(jnp.bfloat16)
        values = jnp.einsum('htc,che->the', o_lat.astype(jnp.float32), wuv.reshape(KR, HEADS_DEV, VD).astype(jnp.float32)).astype(jnp.bfloat16)
        partial_value = jnp.dot(values.reshape(SPAN, HEADS_DEV * VD), wout, preferred_element_type=jnp.float32).astype(jnp.bfloat16)
        return (total + partial_value.astype(jnp.float32), None)
    total, _ = lax.scan(block, jnp.zeros((SPAN, D), jnp.float32), jnp.arange(H // HEADS_DEV, dtype=jnp.int32))
    return total.astype(jnp.bfloat16)
```

```python
import functools

import jax
import jax.numpy as jnp
from jax import lax
from jax.experimental import pallas as pl
from jax.experimental.pallas import tpu as pltpu
from jax.sharding import PartitionSpec as P

KR = 512
RD = 64
ND = 128
VD = 128
CHUNKS = 4
LAG = 2
BF = jnp.bfloat16
F32 = jnp.float32
MESH = pl.DeviceIdType.MESH
NT = (((1,), (1,)), ((), ()))


def ring_place(h, n):
    if n != 8:
        return h
    odd = h % 2
    return (1 - odd) * (h // 2) + odd * (n - 1 - h // 2)


def ring_index(p, n):
    if n != 8:
        return p
    far = p // (n // 2)
    return (1 - far) * (2 * p) + far * (2 * (n - 1 - p) + 1)


def frequencies(shape):
    lane = lax.broadcasted_iota(jnp.int32, shape, 1) % 32
    freq = jnp.ones(shape, F32)
    for bit in range(5):
        factor = 10000.0 ** (-(2.0**bit) / 32.0)
        freq = jnp.where((lane // (2**bit)) % 2 == 1, freq * factor, freq)
    return freq


def dot(a, b):
    return jnp.dot(a, b, preferred_element_type=F32)


def kernel(
    n,
    length_ref,
    gain_ref,
    q_ref,
    new_ref,
    cache_ref,
    wqn_ref,
    wqr_ref,
    wuk_ref,
    wuv_ref,
    wo_ref,
    out_ref,
    q_all,
    new_own,
    kc,
    kf,
    wqn,
    wqr,
    wuk,
    wuv,
    wo,
    qa,
    scores,
    weights,
    o_lat,
    values,
    part,
    rs,
    load_sem,
    own_sem,
    wo_sem,
    q_send,
    q_recv,
    kc_send,
    kc_recv,
    kcs_send,
    kf_send,
    kf_recv,
    kfs_send,
    rs_send,
    rs_recv,
):
    half = n // 2
    core = lax.axis_index("query")
    other = 1 - core
    me = ring_place(lax.axis_index("heads"), n)
    right = {"heads": ring_index((me + 1) % n, n)}
    left = {"heads": ring_index((me + n - 1) % n, n)}
    sibling = {"query": other}
    way = (right, left)
    tok = q_ref.shape[0]
    slots = cache_ref.shape[0]
    piece = slots // 2
    rows = n * tok
    heads = wqn_ref.shape[1] // ND
    ctx = n * 2 * slots
    width = wo.shape[2]

    def source(direction, step):
        return (me + n - step) % n if direction == 0 else (me + step) % n

    own_q = pltpu.make_async_copy(q_ref, q_all.at[me], own_sem.at[0])
    own_new = pltpu.make_async_copy(new_ref, new_own, own_sem.at[1])
    own_cache = [
        pltpu.make_async_copy(
            cache_ref.at[pl.ds(i * piece, piece)], kc.at[me, core, i], own_sem.at[2 + i]
        )
        for i in range(2)
    ]
    own_new.start()
    own_q.start()
    for copy in own_cache:
        copy.start()
    loads = [
        pltpu.make_async_copy(src, dst, load_sem.at[i])
        for i, (src, dst) in enumerate(
            ((wqn_ref, wqn), (wqr_ref, wqr), (wuk_ref, wuk), (wuv_ref, wuv))
        )
    ]
    loads += [
        pltpu.make_async_copy(wo_ref.at[:, pl.ds(i * width, width)], wo.at[i], wo_sem.at[i])
        for i in range(CHUNKS)
    ]
    for copy in loads:
        copy.start()

    barrier = pltpu.get_barrier_semaphore()
    for target in (right, left, sibling):
        pl.semaphore_signal(barrier, inc=1, device_id=target, device_id_type=MESH)

    length = length_ref[0]
    mine = (ring_index(me, n) * 2 + core) * tok
    own_new.wait()
    latent = new_own[:, :KR].astype(F32)
    mean = jnp.mean(latent * latent, axis=-1, keepdims=True)
    latent = latent * lax.rsqrt(mean + 1e-06) * gain_ref[...][None, :]
    turned = new_own[:, KR:].astype(F32)
    position = (length + mine + lax.broadcasted_iota(jnp.int32, (tok, RD), 0)).astype(F32)
    angle = position * frequencies((tok, RD))
    swapped = jnp.concatenate([-turned[:, RD // 2 :], turned[:, : RD // 2]], axis=1)
    turned = turned * jnp.cos(angle) + swapped * jnp.sin(angle)
    kf[me, core, :, :KR] = latent.astype(BF)
    kf[me, core, :, KR:] = turned.astype(BF)

    pl.semaphore_wait(barrier, 3)

    def remote(src, dst, send, recv, target):
        return pltpu.make_async_remote_copy(
            src_ref=src, dst_ref=dst, send_sem=send, recv_sem=recv, device_id=target, device_id_type=MESH
        )

    def q_copy(direction, step, chunk):
        src = q_ref if step == 0 else q_all.at[chunk]
        return remote(
            src, q_all.at[chunk], q_send.at[direction, step], q_recv.at[chunk], way[direction]
        )

    def kc_copy(direction, step, chunk, i):
        src = cache_ref.at[pl.ds(i * piece, piece)] if step == 0 else kc.at[chunk, core, i]
        return remote(
            src,
            kc.at[chunk, core, i],
            kc_send.at[direction, step, i],
            kc_recv.at[core, chunk, i],
            way[direction],
        )

    def kf_copy(direction, step, chunk):
        return remote(
            kf.at[chunk, core],
            kf.at[chunk, core],
            kf_send.at[direction, step],
            kf_recv.at[core, chunk],
            way[direction],
        )

    def kc_across(chunk, i, owner, own=False):
        src = cache_ref.at[pl.ds(i * piece, piece)] if own else kc.at[chunk, owner, i]
        return remote(
            src, kc.at[chunk, owner, i], kcs_send.at[chunk, i], kc_recv.at[owner, chunk, i], sibling
        )

    def kf_across(chunk, owner):
        return remote(
            kf.at[chunk, owner],
            kf.at[chunk, owner],
            kfs_send.at[chunk],
            kf_recv.at[owner, chunk],
            sibling,
        )

    q_hops = (half, half - 1)
    f_hops = (half - 1, half)

    def c_hops(direction, i):
        return half if direction == i else half - 1

    sent = []

    def start(copy):
        copy.start()
        sent.append(copy)

    for d in range(2):
        start(q_copy(d, 0, me))
    for d in range(2):
        start(kf_copy(d, 0, me))
    for i in range(2):
        for d in range(2):
            start(kc_copy(d, 0, me, i))
    start(kf_across(me, core))
    for i in range(2):
        start(kc_across(me, i, core, True))

    def q_step(step):
        for d in range(2):
            if step <= q_hops[d]:
                chunk = source(d, step)
                q_copy(d, step - 1, chunk).wait_recv()
                if step < q_hops[d]:
                    start(q_copy(d, step, chunk))

    def k_step(step):
        for d in range(2):
            chunk = source(d, step)
            if step <= f_hops[d]:
                kf_copy(d, step - 1, chunk).wait_recv()
                if step < f_hops[d]:
                    start(kf_copy(d, step, chunk))
                start(kf_across(chunk, core))
        for i in range(2):
            for d in range(2):
                chunk = source(d, step)
                if step <= c_hops(d, i):
                    kc_copy(d, step - 1, chunk, i).wait_recv()
                    if step < c_hops(d, i):
                        start(kc_copy(d, step, chunk, i))
                    start(kc_across(chunk, i, core))

    for step in range(1, half + 1):
        q_step(step)
        if step > LAG:
            k_step(step - LAG)

    own_q.wait()
    loads[0].wait()
    loads[1].wait()
    q_rows = q_all[...].astype(F32).reshape(rows, q_ref.shape[1]).astype(BF)
    row = lax.broadcasted_iota(jnp.int32, (rows, 1), 0)
    row_token = (ring_index(row // tok, n) * 2 + core) * tok + row % tok
    q_nope = dot(q_rows, wqn[...]).astype(BF)
    rope = dot(q_rows, wqr[...])
    angle = (length + row_token).astype(F32) * frequencies((1, 2 * RD))
    cos = jnp.concatenate([jnp.cos(angle)] * (heads // 2), axis=1)
    sin = jnp.concatenate([jnp.sin(angle)] * (heads // 2), axis=1)
    total = heads * RD
    lane = lax.broadcasted_iota(jnp.int32, (rows, total), 1) % RD
    swapped = jnp.where(
        lane < RD // 2,
        -pltpu.roll(rope, total - RD // 2, 1),
        pltpu.roll(rope, RD // 2, 1),
    )
    rope = (rope * cos + swapped * sin).astype(BF)
    loads[2].wait()
    for h in range(heads):
        span = pl.ds(h * rows, rows)
        wk = wuk[:, h * ND : (h + 1) * ND]
        qa[span, :KR] = lax.dot_general(
            q_nope[:, h * ND : (h + 1) * ND], wk, NT, preferred_element_type=F32
        ).astype(BF)
        qa[span, KR:] = rope[:, h * RD : (h + 1) * RD]

    scale = (ND + RD) ** (-0.5)

    def score(chunk):
        keys = kc[chunk].reshape(2 * slots, KR + RD)
        value = lax.dot_general(qa[...], keys, NT, preferred_element_type=F32) * scale
        kidx = ring_index(chunk, n) * (2 * slots) + lax.broadcasted_iota(
            jnp.int32, (1, 2 * slots), 1
        )
        at = pl.multiple_of(chunk * (2 * slots), 2 * slots)
        scores[:, pl.ds(at, 2 * slots)] = jnp.where(kidx < length, value, -1e30)

    def sibling_step(chunk):
        kf_across(chunk, other).wait_recv()
        for i in range(2):
            kc_across(chunk, i, other).wait_recv()

    for copy in own_cache:
        copy.wait()
    sibling_step(me)
    if n == 8:
        score(me)
    for step in range(1, half + 1):
        if step > half - LAG:
            k_step(step)
        for d in range(2):
            if d == 0 or step < half:
                sibling_step(source(d, step))
                if n == 8:
                    score(source(d, step))
    if n != 8:
        lax.fori_loop(0, n, lambda p, carry: (score(p), carry)[1], 0)

    fresh = kf[...].astype(F32).reshape(2 * rows, KR + RD).astype(BF)
    value = lax.dot_general(qa[...], fresh, NT, preferred_element_type=F32) * scale
    key = lax.broadcasted_iota(jnp.int32, (1, 2 * rows), 1)
    key_token = ring_index(key // (2 * tok), n) * (2 * tok) + key % (2 * tok)
    row = lax.broadcasted_iota(jnp.int32, (heads * rows, 1), 0) % rows
    row_token = (ring_index(row // tok, n) * 2 + core) * tok + row % tok
    scores[:, pl.ds(ctx, 2 * rows)] = jnp.where(key_token <= row_token, value, -1e30)

    block = weights.shape[0]
    strip = 64

    def attend(b, carry):
        base = b * block

        def soften(r, inner):
            s = scores[pl.ds(pl.multiple_of(base + r * strip, strip), strip), :]
            e = jnp.exp(s - jnp.max(s, axis=-1, keepdims=True))
            e = e * (1.0 / jnp.sum(e, axis=-1, keepdims=True))
            weights[pl.ds(pl.multiple_of(r * strip, strip), strip), :] = e.astype(BF)
            return inner

        lax.fori_loop(0, block // strip, soften, 0)
        latents = kc[:, :, :, :, :KR].reshape(ctx, KR)
        o = dot(weights[:, :ctx], latents) + dot(weights[:, ctx:], fresh[:, :KR])
        o_lat[pl.ds(pl.multiple_of(base, block), block), :] = o.astype(BF)
        return carry

    lax.fori_loop(0, heads * rows // block, attend, 0)

    loads[3].wait()
    for h in range(heads):
        values[:, h * VD : (h + 1) * VD] = dot(
            o_lat[pl.ds(h * rows, rows), :], wuv[:, h * VD : (h + 1) * VD]
        ).astype(BF)

    def sum_hops(d, c):
        return half if (d == 0) == (c < CHUNKS // 2) else half - 1

    def toward(d, distance):
        return (me + distance) % n if d == 0 else (me + n - distance) % n

    def rs_copy(d, t, c):
        src = part.at[toward(d, sum_hops(d, c)), c] if t == 0 else rs.at[d, t - 1, c]
        return remote(src, rs.at[d, t, c], rs_send.at[d, t, c], rs_recv.at[d, t, c], way[d])

    for c in range(CHUNKS):
        loads[4 + c].wait()
        value = dot(values[...], wo[c])
        part[:, c] = value.reshape(n, tok, width).astype(BF)
        for d in range(2):
            start(rs_copy(d, 0, c))
    for t in range(1, half + 1):
        for c in range(CHUNKS):
            for d in range(2):
                hops = sum_hops(d, c)
                if t < hops:
                    rs_copy(d, t - 1, c).wait_recv()
                    held = rs[d, t - 1, c].astype(F32) + part[toward(d, hops - t), c].astype(F32)
                    rs[d, t - 1, c] = held.astype(BF)
                    start(rs_copy(d, t, c))
    for c in range(CHUNKS):
        total_value = part[me, c].astype(F32)
        for d in range(2):
            hops = sum_hops(d, c)
            rs_copy(d, hops - 1, c).wait_recv()
            total_value = total_value + rs[d, hops - 1, c].astype(F32)
        out_ref[:, c * width : (c + 1) * width] = total_value.astype(BF)
    for copy in sent:
        copy.wait_send()


def shards(
    n,
    q_compressed,
    new_latent,
    cached_latent,
    latent_gain,
    cached_length,
    w_q_nope,
    w_q_rope,
    w_uk,
    w_uv,
    w_out,
):
    tok, qr = q_compressed.shape
    slots, kw = cached_latent.shape
    heads = w_q_nope.shape[1] // ND
    depth, model = w_out.shape
    rows = n * tok
    ctx = n * 2 * slots
    half = n // 2
    width = model // CHUNKS
    hbm = pl.BlockSpec(memory_space=pl.ANY)
    vmem = pl.BlockSpec(memory_space=pltpu.VMEM)
    dma = pltpu.SemaphoreType.DMA
    block = min(256, heads * rows)
    return pl.pallas_call(
        functools.partial(kernel, n),
        out_shape=jax.ShapeDtypeStruct((tok, model), BF),
        in_specs=[pl.BlockSpec(memory_space=pltpu.SMEM), vmem] + [hbm] * 8,
        out_specs=vmem,
        scratch_shapes=[
            pltpu.VMEM((n, tok, qr), BF),
            pltpu.VMEM((tok, kw), BF),
            pltpu.VMEM((n, 2, 2, slots // 2, kw), BF),
            pltpu.VMEM((n, 2, tok, kw), BF),
            pltpu.VMEM(w_q_nope.shape, BF),
            pltpu.VMEM(w_q_rope.shape, BF),
            pltpu.VMEM(w_uk.shape, BF),
            pltpu.VMEM(w_uv.shape, BF),
            pltpu.VMEM((CHUNKS, depth, width), BF),
            pltpu.VMEM((heads * rows, kw), BF),
            pltpu.VMEM((heads * rows, ctx + 2 * rows), F32),
            pltpu.VMEM((block, ctx + 2 * rows), BF),
            pltpu.VMEM((heads * rows, KR), BF),
            pltpu.VMEM((rows, heads * VD), BF),
            pltpu.VMEM((n, CHUNKS, tok, width), BF),
            pltpu.VMEM((2, half, CHUNKS, tok, width), BF),
            dma((4,)),
            dma((4,)),
            dma((CHUNKS,)),
            dma((2, half)),
            dma((n,)),
            dma((2, half, 2)),
            dma((2, n, 2)),
            dma((n, 2)),
            dma((2, half)),
            dma((2, n)),
            dma((n,)),
            dma((2, half, CHUNKS)),
            dma((2, half, CHUNKS)),
        ],
        compiler_params=pltpu.CompilerParams(
            collective_id=0, has_side_effects=True, vmem_limit_bytes=60 * 1024 * 1024
        ),
    )(
        cached_length,
        latent_gain,
        q_compressed,
        new_latent,
        cached_latent,
        w_q_nope,
        w_q_rope,
        w_uk,
        w_uv,
        w_out,
    )


def solution(mesh):
    placed = (
        P(("groups", "heads", "query"), None),
        P(("groups", "heads", "query"), None),
        P(("groups", "heads", "query"), None),
        P(),
        P("groups"),
        P(None, "heads"),
        P(None, "heads"),
        P(None, "heads"),
        P(None, "heads"),
        P("heads", None),
    )
    return jax.shard_map(
        functools.partial(shards, mesh.shape["heads"]),
        mesh=mesh,
        in_specs=placed,
        out_specs=P(("groups", "heads", "query"), None),
        check_vma=False,
    )
```

```python
import functools

import jax
import jax.numpy as jnp
from jax import lax
from jax.experimental import pallas as pl
from jax.experimental.pallas import tpu as pltpu
from jax.sharding import PartitionSpec as P

KR = 512
RD = 64
ND = 128
VD = 128
CHUNKS = 4
LAG = 1
BF = jnp.bfloat16
F32 = jnp.float32
MESH = pl.DeviceIdType.MESH
NT = (((1,), (1,)), ((), ()))


def ring_place(h, n):
    if n != 8:
        return h
    odd = h % 2
    return (1 - odd) * (h // 2) + odd * (n - 1 - h // 2)


def ring_index(p, n):
    if n != 8:
        return p
    far = p // (n // 2)
    return (1 - far) * (2 * p) + far * (2 * (n - 1 - p) + 1)


def frequencies(shape):
    lane = lax.broadcasted_iota(jnp.int32, shape, 1) % 32
    freq = jnp.ones(shape, F32)
    for bit in range(5):
        factor = 10000.0 ** (-(2.0**bit) / 32.0)
        freq = jnp.where((lane // (2**bit)) % 2 == 1, freq * factor, freq)
    return freq


def dot(a, b):
    return jnp.dot(a, b, preferred_element_type=F32)


def kernel(
    n,
    length_ref,
    gain_ref,
    q_ref,
    new_ref,
    cache_ref,
    wqn_ref,
    wqr_ref,
    wuk_ref,
    wuv_ref,
    wo_ref,
    out_ref,
    q_all,
    new_own,
    kc,
    kf,
    wqn,
    wqr,
    wuk,
    wuv,
    wo,
    qa,
    scores,
    weights,
    o_lat,
    values,
    part,
    rs,
    load_sem,
    own_sem,
    wo_sem,
    q_send,
    q_recv,
    kc_send,
    kc_recv,
    kcs_send,
    kf_send,
    kf_recv,
    kfs_send,
    rs_send,
    rs_recv,
):
    half = n // 2
    core = lax.axis_index("query")
    other = 1 - core
    me = ring_place(lax.axis_index("heads"), n)
    right = {"heads": ring_index((me + 1) % n, n)}
    left = {"heads": ring_index((me + n - 1) % n, n)}
    sibling = {"query": other}
    way = (right, left)
    tok = q_ref.shape[0]
    slots = cache_ref.shape[0]
    piece = slots // 2
    rows = n * tok
    heads = wqn_ref.shape[1] // ND
    ctx = n * 2 * slots
    width = wo.shape[2]

    def source(direction, step):
        return (me + n - step) % n if direction == 0 else (me + step) % n

    own_q = pltpu.make_async_copy(q_ref, q_all.at[me], own_sem.at[0])
    own_new = pltpu.make_async_copy(new_ref, new_own, own_sem.at[1])
    own_cache = [
        pltpu.make_async_copy(
            cache_ref.at[pl.ds(i * piece, piece)], kc.at[me, core, i], own_sem.at[2 + i]
        )
        for i in range(2)
    ]
    own_new.start()
    own_q.start()
    for copy in own_cache:
        copy.start()
    loads = [
        pltpu.make_async_copy(src, dst, load_sem.at[i])
        for i, (src, dst) in enumerate(
            ((wqn_ref, wqn), (wqr_ref, wqr), (wuk_ref, wuk), (wuv_ref, wuv))
        )
    ]
    loads += [
        pltpu.make_async_copy(wo_ref.at[:, pl.ds(i * width, width)], wo.at[i], wo_sem.at[i])
        for i in range(CHUNKS)
    ]

    barrier = pltpu.get_barrier_semaphore()
    for target in (right, left, sibling):
        pl.semaphore_signal(barrier, inc=1, device_id=target, device_id_type=MESH)

    length = length_ref[0]
    mine = (ring_index(me, n) * 2 + core) * tok
    own_new.wait()
    latent = new_own[:, :KR].astype(F32)
    mean = jnp.mean(latent * latent, axis=-1, keepdims=True)
    latent = latent * lax.rsqrt(mean + 1e-06) * gain_ref[...][None, :]
    turned = new_own[:, KR:].astype(F32)
    position = (length + mine + lax.broadcasted_iota(jnp.int32, (tok, RD), 0)).astype(F32)
    angle = position * frequencies((tok, RD))
    swapped = jnp.concatenate([-turned[:, RD // 2 :], turned[:, : RD // 2]], axis=1)
    turned = turned * jnp.cos(angle) + swapped * jnp.sin(angle)
    kf[me, core, :, :KR] = latent.astype(BF)
    kf[me, core, :, KR:] = turned.astype(BF)

    pl.semaphore_wait(barrier, 3)

    def remote(src, dst, send, recv, target):
        return pltpu.make_async_remote_copy(
            src_ref=src, dst_ref=dst, send_sem=send, recv_sem=recv, device_id=target, device_id_type=MESH
        )

    def q_copy(direction, step, chunk):
        src = q_ref if step == 0 else q_all.at[chunk]
        return remote(
            src, q_all.at[chunk], q_send.at[direction, step], q_recv.at[chunk], way[direction]
        )

    def kc_copy(direction, step, chunk, i):
        src = cache_ref.at[pl.ds(i * piece, piece)] if step == 0 else kc.at[chunk, core, i]
        return remote(
            src,
            kc.at[chunk, core, i],
            kc_send.at[direction, step, i],
            kc_recv.at[core, chunk, i],
            way[direction],
        )

    def kf_copy(direction, step, chunk):
        return remote(
            kf.at[chunk, core],
            kf.at[chunk, core],
            kf_send.at[direction, step],
            kf_recv.at[core, chunk],
            way[direction],
        )

    def kc_across(chunk, i, owner, own=False):
        src = cache_ref.at[pl.ds(i * piece, piece)] if own else kc.at[chunk, owner, i]
        return remote(
            src, kc.at[chunk, owner, i], kcs_send.at[chunk, i], kc_recv.at[owner, chunk, i], sibling
        )

    def kf_across(chunk, owner):
        return remote(
            kf.at[chunk, owner],
            kf.at[chunk, owner],
            kfs_send.at[chunk],
            kf_recv.at[owner, chunk],
            sibling,
        )

    q_hops = (half, half - 1)
    f_hops = (half - 1, half)

    def c_hops(direction, i):
        return half if direction == i else half - 1

    sent = []

    def start(copy):
        copy.start()
        sent.append(copy)

    for d in range(2):
        start(q_copy(d, 0, me))
    for d in range(2):
        start(kf_copy(d, 0, me))
    for i in range(2):
        for d in range(2):
            start(kc_copy(d, 0, me, i))
    start(kf_across(me, core))
    for i in range(2):
        start(kc_across(me, i, core, True))

    for copy in loads:
        copy.start()

    def q_step(step):
        for d in range(2):
            if step <= q_hops[d]:
                chunk = source(d, step)
                q_copy(d, step - 1, chunk).wait_recv()
                if step < q_hops[d]:
                    start(q_copy(d, step, chunk))

    def k_step(step):
        for d in range(2):
            chunk = source(d, step)
            if step <= f_hops[d]:
                kf_copy(d, step - 1, chunk).wait_recv()
                if step < f_hops[d]:
                    start(kf_copy(d, step, chunk))
                start(kf_across(chunk, core))
        for i in range(2):
            for d in range(2):
                chunk = source(d, step)
                if step <= c_hops(d, i):
                    kc_copy(d, step - 1, chunk, i).wait_recv()
                    if step < c_hops(d, i):
                        start(kc_copy(d, step, chunk, i))
                    start(kc_across(chunk, i, core))

    for step in range(1, half + 1):
        q_step(step)
        if LAG < step < half:
            k_step(step - LAG)

    own_q.wait()
    loads[0].wait()
    loads[1].wait()
    q_rows = q_all[...].astype(F32).reshape(rows, q_ref.shape[1]).astype(BF)
    row = lax.broadcasted_iota(jnp.int32, (rows, 1), 0)
    row_token = (ring_index(row // tok, n) * 2 + core) * tok + row % tok
    q_nope = dot(q_rows, wqn[...]).astype(BF)
    rope = dot(q_rows, wqr[...])
    k_step(half - 1)
    angle = (length + row_token).astype(F32) * frequencies((1, 2 * RD))
    cos = jnp.concatenate([jnp.cos(angle)] * (heads // 2), axis=1)
    sin = jnp.concatenate([jnp.sin(angle)] * (heads // 2), axis=1)
    total = heads * RD
    lane = lax.broadcasted_iota(jnp.int32, (rows, total), 1) % RD
    swapped = jnp.where(
        lane < RD // 2,
        -pltpu.roll(rope, total - RD // 2, 1),
        pltpu.roll(rope, RD // 2, 1),
    )
    rope = (rope * cos + swapped * sin).astype(BF)
    loads[2].wait()
    for h in range(heads):
        span = pl.ds(h * rows, rows)
        wk = wuk[:, h * ND : (h + 1) * ND]
        qa[span, :KR] = lax.dot_general(
            q_nope[:, h * ND : (h + 1) * ND], wk, NT, preferred_element_type=F32
        ).astype(BF)
        qa[span, KR:] = rope[:, h * RD : (h + 1) * RD]

    scale = (ND + RD) ** (-0.5)

    def score(chunk):
        keys = kc[chunk].reshape(2 * slots, KR + RD)
        value = lax.dot_general(qa[...], keys, NT, preferred_element_type=F32) * scale
        kidx = ring_index(chunk, n) * (2 * slots) + lax.broadcasted_iota(
            jnp.int32, (1, 2 * slots), 1
        )
        at = pl.multiple_of(chunk * (2 * slots), 2 * slots)
        scores[:, pl.ds(at, 2 * slots)] = jnp.where(kidx < length, value, -1e30)

    def sibling_step(chunk):
        kf_across(chunk, other).wait_recv()
        for i in range(2):
            kc_across(chunk, i, other).wait_recv()

    for copy in own_cache:
        copy.wait()
    sibling_step(me)
    if n == 8:
        score(me)
    for step in range(1, half + 1):
        if step > half - LAG:
            k_step(step)
        for d in range(2):
            if d == 0 or step < half:
                sibling_step(source(d, step))
                if n == 8:
                    score(source(d, step))
    if n != 8:
        lax.fori_loop(0, n, lambda p, carry: (score(p), carry)[1], 0)

    fresh = kf[...].astype(F32).reshape(2 * rows, KR + RD).astype(BF)
    value = lax.dot_general(qa[...], fresh, NT, preferred_element_type=F32) * scale
    key = lax.broadcasted_iota(jnp.int32, (1, 2 * rows), 1)
    key_token = ring_index(key // (2 * tok), n) * (2 * tok) + key % (2 * tok)
    row = lax.broadcasted_iota(jnp.int32, (heads * rows, 1), 0) % rows
    row_token = (ring_index(row // tok, n) * 2 + core) * tok + row % tok
    scores[:, pl.ds(ctx, 2 * rows)] = jnp.where(key_token <= row_token, value, -1e30)

    block = weights.shape[0]
    strip = 64

    def attend(b, carry):
        base = b * block

        def soften(r, inner):
            s = scores[pl.ds(pl.multiple_of(base + r * strip, strip), strip), :]
            e = jnp.exp(s - jnp.max(s, axis=-1, keepdims=True))
            e = e * (1.0 / jnp.sum(e, axis=-1, keepdims=True))
            weights[pl.ds(pl.multiple_of(r * strip, strip), strip), :] = e.astype(BF)
            return inner

        lax.fori_loop(0, block // strip, soften, 0)
        latents = kc[:, :, :, :, :KR].reshape(ctx, KR)
        o = dot(weights[:, :ctx], latents) + dot(weights[:, ctx:], fresh[:, :KR])
        o_lat[pl.ds(pl.multiple_of(base, block), block), :] = o.astype(BF)
        return carry

    lax.fori_loop(0, heads * rows // block, attend, 0)

    loads[3].wait()
    for h in range(heads):
        values[:, h * VD : (h + 1) * VD] = dot(
            o_lat[pl.ds(h * rows, rows), :], wuv[:, h * VD : (h + 1) * VD]
        ).astype(BF)

    def sum_hops(d, c):
        return half if (d == 0) == (c < CHUNKS // 2) else half - 1

    def toward(d, distance):
        return (me + distance) % n if d == 0 else (me + n - distance) % n

    def rs_copy(d, t, c):
        src = part.at[toward(d, sum_hops(d, c)), c] if t == 0 else rs.at[d, t - 1, c]
        return remote(src, rs.at[d, t, c], rs_send.at[d, t, c], rs_recv.at[d, t, c], way[d])

    for c in range(CHUNKS):
        loads[4 + c].wait()
        value = dot(values[...], wo[c])
        part[:, c] = value.reshape(n, tok, width).astype(BF)
        for d in range(2):
            start(rs_copy(d, 0, c))
    for t in range(1, half + 1):
        for c in range(CHUNKS):
            for d in range(2):
                hops = sum_hops(d, c)
                if t < hops:
                    rs_copy(d, t - 1, c).wait_recv()
                    held = rs[d, t - 1, c].astype(F32) + part[toward(d, hops - t), c].astype(F32)
                    rs[d, t - 1, c] = held.astype(BF)
                    start(rs_copy(d, t, c))
    for c in range(CHUNKS):
        total_value = part[me, c].astype(F32)
        for d in range(2):
            hops = sum_hops(d, c)
            rs_copy(d, hops - 1, c).wait_recv()
            total_value = total_value + rs[d, hops - 1, c].astype(F32)
        out_ref[:, c * width : (c + 1) * width] = total_value.astype(BF)
    for copy in sent:
        copy.wait_send()


def shards(
    n,
    q_compressed,
    new_latent,
    cached_latent,
    latent_gain,
    cached_length,
    w_q_nope,
    w_q_rope,
    w_uk,
    w_uv,
    w_out,
):
    tok, qr = q_compressed.shape
    slots, kw = cached_latent.shape
    heads = w_q_nope.shape[1] // ND
    depth, model = w_out.shape
    rows = n * tok
    ctx = n * 2 * slots
    half = n // 2
    width = model // CHUNKS
    hbm = pl.BlockSpec(memory_space=pl.ANY)
    vmem = pl.BlockSpec(memory_space=pltpu.VMEM)
    dma = pltpu.SemaphoreType.DMA
    block = min(256, heads * rows)
    return pl.pallas_call(
        functools.partial(kernel, n),
        out_shape=jax.ShapeDtypeStruct((tok, model), BF),
        in_specs=[pl.BlockSpec(memory_space=pltpu.SMEM), vmem] + [hbm] * 8,
        out_specs=vmem,
        scratch_shapes=[
            pltpu.VMEM((n, tok, qr), BF),
            pltpu.VMEM((tok, kw), BF),
            pltpu.VMEM((n, 2, 2, slots // 2, kw), BF),
            pltpu.VMEM((n, 2, tok, kw), BF),
            pltpu.VMEM(w_q_nope.shape, BF),
            pltpu.VMEM(w_q_rope.shape, BF),
            pltpu.VMEM(w_uk.shape, BF),
            pltpu.VMEM(w_uv.shape, BF),
            pltpu.VMEM((CHUNKS, depth, width), BF),
            pltpu.VMEM((heads * rows, kw), BF),
            pltpu.VMEM((heads * rows, ctx + 2 * rows), F32),
            pltpu.VMEM((block, ctx + 2 * rows), BF),
            pltpu.VMEM((heads * rows, KR), BF),
            pltpu.VMEM((rows, heads * VD), BF),
            pltpu.VMEM((n, CHUNKS, tok, width), BF),
            pltpu.VMEM((2, half, CHUNKS, tok, width), BF),
            dma((4,)),
            dma((4,)),
            dma((CHUNKS,)),
            dma((2, half)),
            dma((n,)),
            dma((2, half, 2)),
            dma((2, n, 2)),
            dma((n, 2)),
            dma((2, half)),
            dma((2, n)),
            dma((n,)),
            dma((2, half, CHUNKS)),
            dma((2, half, CHUNKS)),
        ],
        compiler_params=pltpu.CompilerParams(
            collective_id=0, has_side_effects=True, vmem_limit_bytes=60 * 1024 * 1024
        ),
    )(
        cached_length,
        latent_gain,
        q_compressed,
        new_latent,
        cached_latent,
        w_q_nope,
        w_q_rope,
        w_uk,
        w_uv,
        w_out,
    )


def solution(mesh):
    placed = (
        P(("groups", "heads", "query"), None),
        P(("groups", "heads", "query"), None),
        P(("groups", "heads", "query"), None),
        P(),
        P("groups"),
        P(None, "heads"),
        P(None, "heads"),
        P(None, "heads"),
        P(None, "heads"),
        P("heads", None),
    )
    return jax.shard_map(
        functools.partial(shards, mesh.shape["heads"]),
        mesh=mesh,
        in_specs=placed,
        out_specs=P(("groups", "heads", "query"), None),
        check_vma=False,
    )
```

```python
import functools

import jax
import jax.numpy as jnp
from jax import lax
from jax.experimental import pallas as pl
from jax.experimental.pallas import tpu as pltpu
from jax.sharding import PartitionSpec as P

KR = 512
RD = 64
ND = 128
VD = 128
CHUNKS = 8
BEHIND = 5
LAG = 1
BF = jnp.bfloat16
F32 = jnp.float32
MESH = pl.DeviceIdType.MESH
NT = (((1,), (1,)), ((), ()))


def ring_place(h, n):
    if n != 8:
        return h
    odd = h % 2
    return (1 - odd) * (h // 2) + odd * (n - 1 - h // 2)


def ring_index(p, n):
    if n != 8:
        return p
    far = p // (n // 2)
    return (1 - far) * (2 * p) + far * (2 * (n - 1 - p) + 1)


def frequencies(shape):
    lane = lax.broadcasted_iota(jnp.int32, shape, 1) % 32
    freq = jnp.ones(shape, F32)
    for bit in range(5):
        factor = 10000.0 ** (-(2.0**bit) / 32.0)
        freq = jnp.where((lane // (2**bit)) % 2 == 1, freq * factor, freq)
    return freq


def dot(a, b):
    return jnp.dot(a, b, preferred_element_type=F32)


def kernel(
    n,
    length_ref,
    gain_ref,
    q_ref,
    new_ref,
    cache_ref,
    wqn_ref,
    wqr_ref,
    wuk_ref,
    wuv_ref,
    wo_ref,
    out_ref,
    q_all,
    new_own,
    kc,
    kf,
    wqn,
    wqr,
    wuk,
    wuv,
    wo,
    qa,
    scores,
    weights,
    o_lat,
    values,
    part,
    rs,
    load_sem,
    own_sem,
    wo_sem,
    q_send,
    q_recv,
    kc_send,
    kc_recv,
    kcs_send,
    kf_send,
    kf_recv,
    kfs_send,
    rs_send,
    rs_recv,
):
    half = n // 2
    core = lax.axis_index("query")
    other = 1 - core
    me = ring_place(lax.axis_index("heads"), n)
    right = {"heads": ring_index((me + 1) % n, n)}
    left = {"heads": ring_index((me + n - 1) % n, n)}
    sibling = {"query": other}
    way = (right, left)
    tok = q_ref.shape[0]
    slots = cache_ref.shape[0]
    piece = slots // 2
    rows = n * tok
    heads = wqn_ref.shape[1] // ND
    ctx = n * 2 * slots
    width = wo.shape[2]

    def source(direction, step):
        return (me + n - step) % n if direction == 0 else (me + step) % n

    own_q = pltpu.make_async_copy(q_ref, q_all.at[me], own_sem.at[0])
    own_new = pltpu.make_async_copy(new_ref, new_own, own_sem.at[1])
    own_cache = [
        pltpu.make_async_copy(
            cache_ref.at[pl.ds(i * piece, piece)], kc.at[me, core, i], own_sem.at[2 + i]
        )
        for i in range(2)
    ]
    own_new.start()
    own_q.start()
    for copy in own_cache:
        copy.start()
    loads = [
        pltpu.make_async_copy(src, dst, load_sem.at[i])
        for i, (src, dst) in enumerate(
            ((wqn_ref, wqn), (wqr_ref, wqr), (wuk_ref, wuk), (wuv_ref, wuv))
        )
    ]
    loads += [
        pltpu.make_async_copy(wo_ref.at[:, pl.ds(i * width, width)], wo.at[i], wo_sem.at[i])
        for i in range(CHUNKS)
    ]

    barrier = pltpu.get_barrier_semaphore()
    for target in (right, left, sibling):
        pl.semaphore_signal(barrier, inc=1, device_id=target, device_id_type=MESH)

    length = length_ref[0]
    mine = (ring_index(me, n) * 2 + core) * tok
    own_new.wait()
    latent = new_own[:, :KR].astype(F32)
    mean = jnp.mean(latent * latent, axis=-1, keepdims=True)
    latent = latent * lax.rsqrt(mean + 1e-06) * gain_ref[...][None, :]
    turned = new_own[:, KR:].astype(F32)
    position = (length + mine + lax.broadcasted_iota(jnp.int32, (tok, RD), 0)).astype(F32)
    angle = position * frequencies((tok, RD))
    swapped = jnp.concatenate([-turned[:, RD // 2 :], turned[:, : RD // 2]], axis=1)
    turned = turned * jnp.cos(angle) + swapped * jnp.sin(angle)
    kf[me, core, :, :KR] = latent.astype(BF)
    kf[me, core, :, KR:] = turned.astype(BF)

    pl.semaphore_wait(barrier, 3)

    def remote(src, dst, send, recv, target):
        return pltpu.make_async_remote_copy(
            src_ref=src, dst_ref=dst, send_sem=send, recv_sem=recv, device_id=target, device_id_type=MESH
        )

    def q_copy(direction, step, chunk):
        src = q_ref if step == 0 else q_all.at[chunk]
        return remote(
            src, q_all.at[chunk], q_send.at[direction, step], q_recv.at[chunk], way[direction]
        )

    def kc_copy(direction, step, chunk, i):
        src = cache_ref.at[pl.ds(i * piece, piece)] if step == 0 else kc.at[chunk, core, i]
        return remote(
            src,
            kc.at[chunk, core, i],
            kc_send.at[direction, step, i],
            kc_recv.at[core, chunk, i],
            way[direction],
        )

    def kf_copy(direction, step, chunk):
        return remote(
            kf.at[chunk, core],
            kf.at[chunk, core],
            kf_send.at[direction, step],
            kf_recv.at[core, chunk],
            way[direction],
        )

    def kc_across(chunk, i, owner, own=False):
        src = cache_ref.at[pl.ds(i * piece, piece)] if own else kc.at[chunk, owner, i]
        return remote(
            src, kc.at[chunk, owner, i], kcs_send.at[chunk, i], kc_recv.at[owner, chunk, i], sibling
        )

    def kf_across(chunk, owner):
        return remote(
            kf.at[chunk, owner],
            kf.at[chunk, owner],
            kfs_send.at[chunk],
            kf_recv.at[owner, chunk],
            sibling,
        )

    q_hops = (half, half - 1)
    f_hops = (half - 1, half)

    def c_hops(direction, i):
        return half if direction == i else half - 1

    sent = []

    def start(copy):
        copy.start()
        sent.append(copy)

    for d in range(2):
        start(q_copy(d, 0, me))
    for d in range(2):
        start(kf_copy(d, 0, me))
    for i in range(2):
        for d in range(2):
            start(kc_copy(d, 0, me, i))
    start(kf_across(me, core))
    for i in range(2):
        start(kc_across(me, i, core, True))

    for copy in loads:
        copy.start()

    def q_step(step):
        for d in range(2):
            if step <= q_hops[d]:
                chunk = source(d, step)
                q_copy(d, step - 1, chunk).wait_recv()
                if step < q_hops[d]:
                    start(q_copy(d, step, chunk))

    def k_step(step):
        for d in range(2):
            chunk = source(d, step)
            if step <= f_hops[d]:
                kf_copy(d, step - 1, chunk).wait_recv()
                if step < f_hops[d]:
                    start(kf_copy(d, step, chunk))
                start(kf_across(chunk, core))
        for i in range(2):
            for d in range(2):
                chunk = source(d, step)
                if step <= c_hops(d, i):
                    kc_copy(d, step - 1, chunk, i).wait_recv()
                    if step < c_hops(d, i):
                        start(kc_copy(d, step, chunk, i))
                    start(kc_across(chunk, i, core))

    for step in range(1, half + 1):
        q_step(step)
        if LAG < step < half:
            k_step(step - LAG)

    own_q.wait()
    loads[0].wait()
    loads[1].wait()
    q_rows = q_all[...].astype(F32).reshape(rows, q_ref.shape[1]).astype(BF)
    row = lax.broadcasted_iota(jnp.int32, (rows, 1), 0)
    row_token = (ring_index(row // tok, n) * 2 + core) * tok + row % tok
    q_nope = dot(q_rows, wqn[...]).astype(BF)
    rope = dot(q_rows, wqr[...])
    k_step(half - 1)
    angle = (length + row_token).astype(F32) * frequencies((1, 2 * RD))
    cos = jnp.concatenate([jnp.cos(angle)] * (heads // 2), axis=1)
    sin = jnp.concatenate([jnp.sin(angle)] * (heads // 2), axis=1)
    total = heads * RD
    lane = lax.broadcasted_iota(jnp.int32, (rows, total), 1) % RD
    swapped = jnp.where(
        lane < RD // 2,
        -pltpu.roll(rope, total - RD // 2, 1),
        pltpu.roll(rope, RD // 2, 1),
    )
    rope = (rope * cos + swapped * sin).astype(BF)
    loads[2].wait()
    for h in range(heads):
        span = pl.ds(h * rows, rows)
        wk = wuk[:, h * ND : (h + 1) * ND]
        qa[span, :KR] = lax.dot_general(
            q_nope[:, h * ND : (h + 1) * ND], wk, NT, preferred_element_type=F32
        ).astype(BF)
        qa[span, KR:] = rope[:, h * RD : (h + 1) * RD]

    scale = (ND + RD) ** (-0.5)

    def score(chunk):
        keys = kc[chunk].reshape(2 * slots, KR + RD)
        value = lax.dot_general(qa[...], keys, NT, preferred_element_type=F32) * scale
        kidx = ring_index(chunk, n) * (2 * slots) + lax.broadcasted_iota(
            jnp.int32, (1, 2 * slots), 1
        )
        at = pl.multiple_of(chunk * (2 * slots), 2 * slots)
        scores[:, pl.ds(at, 2 * slots)] = jnp.where(kidx < length, value, -1e30)

    def sibling_step(chunk):
        kf_across(chunk, other).wait_recv()
        for i in range(2):
            kc_across(chunk, i, other).wait_recv()

    for copy in own_cache:
        copy.wait()
    sibling_step(me)
    if n == 8:
        score(me)
    for step in range(1, half + 1):
        if step > half - LAG:
            k_step(step)
        for d in range(2):
            if d == 0 or step < half:
                sibling_step(source(d, step))
                if n == 8:
                    score(source(d, step))
    if n != 8:
        lax.fori_loop(0, n, lambda p, carry: (score(p), carry)[1], 0)

    fresh = kf[...].astype(F32).reshape(2 * rows, KR + RD).astype(BF)
    value = lax.dot_general(qa[...], fresh, NT, preferred_element_type=F32) * scale
    key = lax.broadcasted_iota(jnp.int32, (1, 2 * rows), 1)
    key_token = ring_index(key // (2 * tok), n) * (2 * tok) + key % (2 * tok)
    row = lax.broadcasted_iota(jnp.int32, (heads * rows, 1), 0) % rows
    row_token = (ring_index(row // tok, n) * 2 + core) * tok + row % tok
    scores[:, pl.ds(ctx, 2 * rows)] = jnp.where(key_token <= row_token, value, -1e30)

    block = weights.shape[0]
    strip = 64

    def attend(b, carry):
        base = b * block

        def soften(r, inner):
            s = scores[pl.ds(pl.multiple_of(base + r * strip, strip), strip), :]
            e = jnp.exp(s - jnp.max(s, axis=-1, keepdims=True))
            e = e * (1.0 / jnp.sum(e, axis=-1, keepdims=True))
            weights[pl.ds(pl.multiple_of(r * strip, strip), strip), :] = e.astype(BF)
            return inner

        lax.fori_loop(0, block // strip, soften, 0)
        latents = kc[:, :, :, :, :KR].reshape(ctx, KR)
        o = dot(weights[:, :ctx], latents) + dot(weights[:, ctx:], fresh[:, :KR])
        o_lat[pl.ds(pl.multiple_of(base, block), block), :] = o.astype(BF)
        return carry

    lax.fori_loop(0, heads * rows // block, attend, 0)

    loads[3].wait()
    for h in range(heads):
        values[:, h * VD : (h + 1) * VD] = dot(
            o_lat[pl.ds(h * rows, rows), :], wuv[:, h * VD : (h + 1) * VD]
        ).astype(BF)

    def sum_hops(d, c):
        return half if (d == 0) == (c < CHUNKS // 2) else half - 1

    def toward(d, distance):
        return (me + distance) % n if d == 0 else (me + n - distance) % n

    def rs_copy(d, t, c):
        src = part.at[toward(d, sum_hops(d, c)), c] if t == 0 else rs.at[d, t - 1, c]
        return remote(src, rs.at[d, t, c], rs_send.at[d, t, c], rs_recv.at[d, t, c], way[d])

    def pass_on(t, c):
        for d in range(2):
            hops = sum_hops(d, c)
            if t < hops:
                rs_copy(d, t - 1, c).wait_recv()
                held = rs[d, t - 1, c].astype(F32) + part[toward(d, hops - t), c].astype(F32)
                rs[d, t - 1, c] = held.astype(BF)
                start(rs_copy(d, t, c))

    for c in range(CHUNKS):
        loads[4 + c].wait()
        value = dot(values[...], wo[c])
        part[:, c] = value.reshape(n, tok, width).astype(BF)
        for d in range(2):
            start(rs_copy(d, 0, c))
        if c >= BEHIND:
            pass_on(1, c - BEHIND)
    for t in range(1, half + 1):
        for c in range(CHUNKS - BEHIND if t == 1 else 0, CHUNKS):
            pass_on(t, c)
    for c in range(CHUNKS):
        total_value = part[me, c].astype(F32)
        for d in range(2):
            hops = sum_hops(d, c)
            rs_copy(d, hops - 1, c).wait_recv()
            total_value = total_value + rs[d, hops - 1, c].astype(F32)
        out_ref[:, c * width : (c + 1) * width] = total_value.astype(BF)
    for copy in sent:
        copy.wait_send()


def shards(
    n,
    q_compressed,
    new_latent,
    cached_latent,
    latent_gain,
    cached_length,
    w_q_nope,
    w_q_rope,
    w_uk,
    w_uv,
    w_out,
):
    tok, qr = q_compressed.shape
    slots, kw = cached_latent.shape
    heads = w_q_nope.shape[1] // ND
    depth, model = w_out.shape
    rows = n * tok
    ctx = n * 2 * slots
    half = n // 2
    width = model // CHUNKS
    hbm = pl.BlockSpec(memory_space=pl.ANY)
    vmem = pl.BlockSpec(memory_space=pltpu.VMEM)
    dma = pltpu.SemaphoreType.DMA
    block = min(256, heads * rows)
    return pl.pallas_call(
        functools.partial(kernel, n),
        out_shape=jax.ShapeDtypeStruct((tok, model), BF),
        in_specs=[pl.BlockSpec(memory_space=pltpu.SMEM), vmem] + [hbm] * 8,
        out_specs=vmem,
        scratch_shapes=[
            pltpu.VMEM((n, tok, qr), BF),
            pltpu.VMEM((tok, kw), BF),
            pltpu.VMEM((n, 2, 2, slots // 2, kw), BF),
            pltpu.VMEM((n, 2, tok, kw), BF),
            pltpu.VMEM(w_q_nope.shape, BF),
            pltpu.VMEM(w_q_rope.shape, BF),
            pltpu.VMEM(w_uk.shape, BF),
            pltpu.VMEM(w_uv.shape, BF),
            pltpu.VMEM((CHUNKS, depth, width), BF),
            pltpu.VMEM((heads * rows, kw), BF),
            pltpu.VMEM((heads * rows, ctx + 2 * rows), F32),
            pltpu.VMEM((block, ctx + 2 * rows), BF),
            pltpu.VMEM((heads * rows, KR), BF),
            pltpu.VMEM((rows, heads * VD), BF),
            pltpu.VMEM((n, CHUNKS, tok, width), BF),
            pltpu.VMEM((2, half, CHUNKS, tok, width), BF),
            dma((4,)),
            dma((4,)),
            dma((CHUNKS,)),
            dma((2, half)),
            dma((n,)),
            dma((2, half, 2)),
            dma((2, n, 2)),
            dma((n, 2)),
            dma((2, half)),
            dma((2, n)),
            dma((n,)),
            dma((2, half, CHUNKS)),
            dma((2, half, CHUNKS)),
        ],
        compiler_params=pltpu.CompilerParams(
            collective_id=0, has_side_effects=True, vmem_limit_bytes=60 * 1024 * 1024
        ),
    )(
        cached_length,
        latent_gain,
        q_compressed,
        new_latent,
        cached_latent,
        w_q_nope,
        w_q_rope,
        w_uk,
        w_uv,
        w_out,
    )


def solution(mesh):
    placed = (
        P(("groups", "heads", "query"), None),
        P(("groups", "heads", "query"), None),
        P(("groups", "heads", "query"), None),
        P(),
        P("groups"),
        P(None, "heads"),
        P(None, "heads"),
        P(None, "heads"),
        P(None, "heads"),
        P("heads", None),
    )
    return jax.shard_map(
        functools.partial(shards, mesh.shape["heads"]),
        mesh=mesh,
        in_specs=placed,
        out_specs=P(("groups", "heads", "query"), None),
        check_vma=False,
    )
```
